256 devices in a mesh: grp: 4 (over x), wide: 64 (over y, z, core).
Axes of the slice: x: 4, y: 4, z: 8, core: 2. Of those that a mesh axis runs over, the one named last changes fastest.
Arguments:
- embeddings: float32 [393216, 768], P(('grp', 'wide')), may hold values from -200 to 200, as said below
Outputs:
- whitened: float32 [393216, 768], P(('grp', 'wide'))
- factor_scaled: float32 [768, 768], replicated
The draws below stay inside these ranges and needn't reach their ends.
Inputs may be any that keep to these rules, and one draw needn't show every extreme that they name: `embeddings`: Real-valued rows; no structure is promised.
All inputs are finite; a program needn't handle non-finite values.
Results may differ from the reference program's by a relative error of at most 0.000054.
Values sent between devices are 32-bit elements; how exact they have to be, the bound alone decides.
A program may use at most 128 MiB of HBM per device.

```python
import math
import jax
import jax.numpy as jnp
from jax import lax

W = 768
ROWS = 393216


def draw_embeddings(key, part):
    key = jax.random.fold_in(key, 1)
    key_scale, key_offset, key_noise = jax.random.split(key, 3)
    top = math.log(10.0)
    noise = jnp.clip(jax.random.normal(key_noise, (ROWS, W), jnp.float32), -6.0, 6.0)
    col_scale = jnp.exp(jax.random.uniform(key_scale, (W,), jnp.float32, 0.0, top))
    offsets = jax.random.uniform(key_offset, (W,), jnp.float32, -3.0, 3.0)
    position = jnp.arange(ROWS, dtype=jnp.float32) / ROWS
    row_scale = 1.0 + 2.0 * position
    return offsets[None, :] + row_scale[:, None] * col_scale[None, :] * noise


def setup_inputs(seed: int = 0) -> dict:
    key_of = jax.random.split(jax.random.key(seed), 2)
    embeddings = draw_embeddings(jax.random.fold_in(key_of[1], 71), 0)
    return {"embeddings": embeddings}


def reference(embeddings):
    row_count = embeddings.shape[0]
    col_mean = lax.optimization_barrier(jnp.sum(embeddings, axis=0)) / row_count
    centred = embeddings - col_mean[None, :]
    gram = lax.dot_general(centred.astype(jnp.float32), centred.astype(jnp.float32), (((0,), (0,)), ((), ())), precision=lax.Precision.HIGHEST, preferred_element_type=jnp.float32)
    lower = jnp.linalg.cholesky(gram)
    factor = lower.T
    scale = jnp.sqrt(jnp.float32(row_count))
    solved = jax.scipy.linalg.solve_triangular(lower, centred.T, lower=True)
    whitened = solved.T * scale
    return (whitened, factor / scale)
```

```python
import functools
import math

import jax
import jax.numpy as jnp
from jax import lax
from jax.experimental import pallas as pl
from jax.experimental.pallas import tpu as pltpu
from jax.sharding import PartitionSpec as P

F32 = jnp.float32
BF16 = jnp.bfloat16
HI = lax.Precision.HIGHEST
MESH = pl.DeviceIdType.MESH
B = 128
TT = (((0,), (0,)), ((), ()))
NT = (((1,), (1,)), ((), ()))


def tri_blocks(nb):
    return [(i, j) for i in range(nb) for j in range(i, nb)]


def split(x):
    hi = x.astype(BF16)
    return hi, (x - hi.astype(F32)).astype(BF16)


def gram_kernel(
    dims,
    x_ref,
    g_ref,
    mean_ref,
    hi,
    lo,
    own,
    from_core,
    a_in,
    b_own,
    b_in,
    z_own,
    z_in,
    z_all,
    b_all,
    mbuf,
    m_in,
    ssem,
    rsem,
):
    nx, ny, nz, width = dims
    rows = x_ref.shape[0]
    nb = width // B
    blocks = tri_blocks(nb)
    at = {ij: k for k, ij in enumerate(blocks)}

    mx = lax.axis_index("grp")
    wide = lax.axis_index("wide")
    mc = lax.rem(wide, 2)
    chip = wide // 2
    mz = lax.rem(chip, nz)
    my = chip // nz

    def dev(x, y, z, c):
        return (x, (y * nz + z) * 2 + c)

    def x_peer(d):
        return dev(lax.rem(mx + d, nx), my, mz, mc)

    def y_peer(d):
        return dev(mx, lax.rem(my + d, ny), mz, mc)

    def z_peer(d):
        return dev(mx, my, lax.rem(mz + d, nz), mc)

    core_peer = dev(mx, my, mz, 1 - mc)
    everyone = (
        [core_peer]
        + [x_peer(d) for d in range(1, nx)]
        + [y_peer(d) for d in range(1, ny)]
        + [z_peer(d) for d in range(1, nz)]
    )
    barrier = pltpu.get_barrier_semaphore()
    for who in everyone:
        pl.semaphore_signal(barrier, inc=1, device_id=who, device_id_type=MESH)

    counter = [0]

    def send(src, dst, who):
        k = counter[0]
        counter[0] += 1
        copy = pltpu.make_async_remote_copy(
            src_ref=src,
            dst_ref=dst,
            send_sem=ssem.at[k],
            recv_sem=rsem.at[k],
            device_id=who,
            device_id_type=MESH,
        )
        copy.start()
        sent.append(copy)
        return copy

    sent = []

    total = jnp.sum(x_ref[...], axis=0, keepdims=True)
    local = total * (1.0 / rows)
    mbuf[0] = jnp.zeros((8, B), F32)
    for i in range(nb):
        mbuf[0, i : i + 1, :] = local[:, i * B : (i + 1) * B]

    pl.semaphore_wait(barrier, len(everyone))

    def mean_phase(stage, peers, base):
        copies = [
            send(mbuf.at[stage], m_in.at[base + d], who) for d, who in enumerate(peers)
        ]

        def finish():
            acc = mbuf[stage]
            for d, copy in enumerate(copies):
                copy.wait_recv()
                acc = acc + m_in[base + d]
            mbuf[stage + 1] = acc

        return finish

    stages = [
        [core_peer],
        [x_peer(d) for d in range(1, nx)],
        [y_peer(d) for d in range(1, ny)],
        [z_peer(d) for d in range(1, nz)],
    ]
    base = 0
    finish = mean_phase(0, stages[0], base)
    base += 1
    centred = x_ref[...] - local
    h, l = split(centred)
    hi[...] = h
    lo[...] = l

    for part in range(3):
        finish()
        finish = mean_phase(part + 1, stages[part + 1], base)
        base += len(stages[part + 1])
        top = 2 * B * (part + 1)
        cols = slice(2 * B * part, top)
        g = lax.dot_general(hi[:, :top], hi[:, cols], TT, preferred_element_type=F32)
        g += lax.dot_general(hi[:, :top], lo[:, cols], TT, preferred_element_type=F32)
        g += lax.dot_general(lo[:, :top], hi[:, cols], TT, preferred_element_type=F32)
        g += lax.dot_general(lo[:, :top], lo[:, cols], TT, preferred_element_type=F32)
        for j in (2 * part, 2 * part + 1):
            for i in range(j + 1):
                off = (j - 2 * part) * B
                own[at[i, j]] = g[i * B : (i + 1) * B, off : off + B]
    finish()
    count = nx * ny * nz * 2
    mean8 = mbuf[4] * (1.0 / count)
    for i in range(nb):
        mean_ref[:, i * B : (i + 1) * B] = mean8[i : i + 1, :]
    delta = mbuf[0] - mean8
    delta_t = delta.T * float(rows)
    for i in range(nb):
        col = jnp.broadcast_to(delta_t[:, i : i + 1], (B, B))
        for j in range(i, nb):
            row = jnp.broadcast_to(delta[j : j + 1, :], (B, B))
            own[at[i, j]] = own[at[i, j]] + col * row

    own_t = own.reshape(2, 2, nx, -1, B)
    core_t = from_core.reshape(2, nx, -1, B)
    ta = own_t.shape[3]
    g_t = g_ref.reshape(2, 2, nx, ta, B)
    tb = b_in.shape[2]

    core_copies = [
        [
            send(own_t.at[1 - mc, q, k], core_t.at[q, k], core_peer)
            for q in range(2)
        ]
        for k in range(nx)
    ]
    core_copies = [[core_copies[k][q] for k in range(nx)] for q in range(2)]
    ax = [(x_peer, mx), (y_peer, my)]
    a_copies = [[], []]
    for c in core_copies[0] + core_copies[1]:
        c.wait_recv()
    for d in list(range(1, nx)) + [0]:
        for q in range(2):
            peer, me = ax[q]
            k = lax.rem(me + d, nx)
            own_t[mc, q, k] = own_t[mc, q, k] + core_t[q, k]
            if d:
                a_copies[q].append(send(own_t.at[mc, q, k], a_in.at[q, d - 1], peer(d)))
    b_copies = [[], []]
    for q in range(2):
        me = ax[q][1]
        acc = own_t[mc, q, me]
        for d in range(1, nx):
            a_copies[q][d - 1].wait_recv()
            acc = acc + a_in[q, d - 1]
        b_own[q, 0:ta] = acc
        b_own[q, ta:] = jnp.zeros((b_own.shape[1] - ta, B), F32)
        peer, me = ax[1 - q]
        for d in range(1, ny):
            k = lax.rem(me + d, ny)
            b_copies[q].append(
                send(
                    b_own.at[q, pl.ds(pl.multiple_of(k * tb, 8), tb)],
                    b_in.at[q, d - 1],
                    peer(d),
                )
            )
    for q in range(2):
        me = ax[1 - q][1]
        acc = b_own[q, pl.ds(pl.multiple_of(me * tb, 8), tb)]
        for d in range(1, ny):
            b_copies[q][d - 1].wait_recv()
            acc = acc + b_in[q, d - 1]
        z_own[q * tb : (q + 1) * tb] = acc
    tz = z_in.shape[1]
    z_own[2 * tb :] = jnp.zeros((z_own.shape[0] - 2 * tb, B), F32)
    z_copies = []
    for d in range(1, nz):
        k = lax.rem(mz + d, nz)
        z_copies.append(
            send(z_own.at[pl.ds(pl.multiple_of(k * tz, 8), tz)], z_in.at[d - 1], z_peer(d))
        )
    acc = z_own[pl.ds(pl.multiple_of(mz * tz, 8), tz)]
    for d in range(1, nz):
        z_copies[d - 1].wait_recv()
        acc = acc + z_in[d - 1]
    mine = pl.ds(pl.multiple_of(mz * tz, 8), tz)
    z_all[mine] = acc
    z_copies = [send(z_all.at[mine], z_all.at[mine], z_peer(d)) for d in range(1, nz)]
    for c in z_copies:
        c.wait_recv()
    b_copies = [[], []]
    for q in range(2):
        peer, me = ax[1 - q]
        mine = pl.ds(pl.multiple_of(me * tb, 8), tb)
        src = z_all.at[q * tb : (q + 1) * tb]
        b_copies[q] = [send(src, b_all.at[q, mine], peer(d)) for d in range(1, ny)]
        b_all[q, mine] = z_all[q * tb : (q + 1) * tb]
    a_copies = [[], []]
    core_copies = []
    for q in range(2):
        for c in b_copies[q]:
            c.wait_recv()
        peer, me = ax[q]
        src = b_all.at[q, 0:ta]
        a_copies[q] = [send(src, g_t.at[mc, q, me], peer(d)) for d in range(1, nx)]
        core_copies.append(send(src, g_t.at[mc, q, me], core_peer))
        g_t[mc, q, me] = b_all[q, 0:ta]
    for d in range(1, nx):
        for q in range(2):
            a_copies[q][d - 1].wait_recv()
            k = lax.rem(ax[q][1] + nx - d, nx)
            core_copies.append(send(g_t.at[mc, q, k], g_t.at[mc, q, k], core_peer))
    for c in core_copies:
        c.wait_recv()
    for c in sent:
        c.wait_send()


def summed_gram(dims, x):
    nx, ny, nz, width = dims
    rows = x.shape[0]
    nb = width // B
    n_blocks = nb * (nb + 1) // 2
    total = n_blocks * B
    ta = total // (4 * nx)
    tb = -(-ta // (8 * ny)) * 8
    tz = -(-2 * tb // (8 * nz)) * 8
    n_mean = 1 + (nx - 1) + (ny - 1) + (nz - 1)
    n_copies = n_mean + 2 * (2 * nx + 2 * (nx - 1) + 2 * (ny - 1) + nz - 1)
    vmem = pl.BlockSpec(memory_space=pltpu.VMEM)
    return pl.pallas_call(
        functools.partial(gram_kernel, dims),
        out_shape=(
            jax.ShapeDtypeStruct((n_blocks, B, B), F32),
            jax.ShapeDtypeStruct((1, width), F32),
        ),
        in_specs=[vmem],
        out_specs=(vmem, vmem),
        scratch_shapes=[
            pltpu.VMEM((rows, width), BF16),
            pltpu.VMEM((rows, width), BF16),
            pltpu.VMEM((n_blocks, B, B), F32),
            pltpu.VMEM((total // 2, B), F32),
            pltpu.VMEM((2, nx - 1, ta, B), F32),
            pltpu.VMEM((2, tb * ny, B), F32),
            pltpu.VMEM((2, ny - 1, tb, B), F32),
            pltpu.VMEM((tz * nz, B), F32),
            pltpu.VMEM((nz - 1, tz, B), F32),
            pltpu.VMEM((tz * nz, B), F32),
            pltpu.VMEM((2, tb * ny, B), F32),
            pltpu.VMEM((5, 8, B), F32),
            pltpu.VMEM((n_mean, 8, B), F32),
            pltpu.SemaphoreType.DMA((n_copies,)),
            pltpu.SemaphoreType.DMA((n_copies,)),
        ],
        compiler_params=pltpu.CompilerParams(
            collective_id=0, has_side_effects=True, vmem_limit_bytes=56 << 20
        ),
        cost_estimate=pl.CostEstimate(
            flops=2 * rows * width * width, bytes_accessed=4 * rows * width, transcendentals=0
        ),
        name="summed_gram",
    )(x)


def rows_bcast(x, k):
    return jnp.broadcast_to(x[k : k + 1, :], (8, B))


def lane_bcast(x, c):
    return jnp.broadcast_to(x[:, c : c + 1], (8, B))


def factor_block(S):
    lane = lax.broadcasted_iota(jnp.int32, (8, B), 1)
    sub = lax.broadcasted_iota(jnp.int32, (8, B), 0)
    S = list(S)
    out = []
    for p in range(16):
        base = 8 * p
        inpanel = (lane >= base) & (lane < base + 8)
        cols = [lane_bcast(S[p], base + j) for j in range(8)]
        D = {(k, j): rows_bcast(cols[j], k) for j in range(8) for k in range(j + 1)}
        row = [
            jnp.where(inpanel, jnp.where(lane == base + k, 1.0, 0.0), rows_bcast(S[p], k))
            for k in range(8)
        ]
        m = {}
        r = [None] * 8
        for j in range(8):
            r[j] = 1.0 / D[j, j]
            for k in range(j + 1, 8):
                m[j, k] = D[j, k] * r[j]
                for l in range(k, 8):
                    D[k, l] = D[k, l] - m[j, k] * D[j, l]
                row[k] = row[k] - m[j, k] * row[j]
        rs = [lax.rsqrt(D[j, j]) for j in range(8)]
        v = [row[j] * r[j] for j in range(8)]
        q = list(v)
        for k in range(6, -1, -1):
            for l in range(k + 1, 8):
                q[k] = q[k] - m[k, l] * q[l]
        o = jnp.zeros((8, B), F32)
        for k in range(8):
            rk = row[k] * rs[k]
            for l in range(k + 1, 8):
                rk = jnp.where(lane == base + l, D[k, l] * rs[k], rk)
            o = jnp.where(sub == k, rk, o)
        out.append(o)
        for i in range(p + 1, 16):
            c = [lane_bcast(S[i], base + j) for j in range(8)]
            acc = jnp.where(inpanel, 0.0, S[i])
            if i == p + 1:
                for k in range(1, 8):
                    for j in range(k):
                        c[k] = c[k] - c[j] * m[j, k]
                for j in range(8):
                    acc = acc - c[j] * v[j]
            else:
                for j in range(8):
                    acc = acc - c[j] * q[j]
            S[i] = acc
    return out


def factor_kernel(scale, g_ref, r_ref, mh_ref, ml_ref, w_ref):
    n = r_ref.shape[0]
    nb = n // B
    for k, (i, j) in enumerate(tri_blocks(nb)):
        w_ref[i * B : (i + 1) * B, j * B : (j + 1) * B] = g_ref[k]
    li = lax.broadcasted_iota(jnp.int32, (B, B), 0)
    lj = lax.broadcasted_iota(jnp.int32, (B, B), 1)

    def dot(a, b):
        return jnp.dot(a, b, precision=HI, preferred_element_type=F32)

    def dot_t(a, b):
        return lax.dot_general(a, b, TT, precision=HI, preferred_element_type=F32)

    for b in range(nb):
        bs = slice(B * b, B * (b + 1))
        S = [w_ref[B * b + 8 * i : B * b + 8 * i + 8, bs] for i in range(16)]
        for i, o in enumerate(factor_block(S)):
            w_ref[B * b + 8 * i : B * b + 8 * i + 8, bs] = o
        F = w_ref[bs, bs]
        M = jnp.where(li >= lj, F, 0.0)
        before = slice(0, B * b)
        after = slice(B * (b + 1), n)
        if b > 0:
            w_ref[bs, before] = dot(M, w_ref[bs, before])
        if b < nb - 1:
            w_ref[bs, after] = dot(M, w_ref[bs, after])
        for i in range(b + 1, nb):
            s = slice(B * i, B * (i + 1))
            rest = slice(B * i, n)
            Rt = w_ref[bs, s]
            w_ref[s, rest] = w_ref[s, rest] - dot_t(Rt, w_ref[bs, rest])
            if b > 0:
                w_ref[s, before] = w_ref[s, before] - dot_t(Rt, w_ref[bs, before])
            w_ref[s, bs] = -dot_t(Rt, M)
        inv = 1.0 / scale
        R = jnp.where(li < lj, F, jnp.where(li == lj, 1.0 / F, 0.0))
        r_ref[bs, bs] = R * inv
        h, l = split(M * scale)
        mh_ref[bs, bs] = h
        ml_ref[bs, bs] = l
        if b > 0:
            r_ref[bs, before] = jnp.zeros((B, B * b), F32)
            h, l = split(w_ref[bs, before] * scale)
            mh_ref[bs, before] = h
            ml_ref[bs, before] = l
        if b < nb - 1:
            r_ref[bs, after] = w_ref[bs, after] * inv
            mh_ref[bs, after] = jnp.zeros((B, n - B * (b + 1)), BF16)
            ml_ref[bs, after] = jnp.zeros((B, n - B * (b + 1)), BF16)


def factor(gram, width, scale):
    vmem = pl.BlockSpec(memory_space=pltpu.VMEM)
    return pl.pallas_call(
        functools.partial(factor_kernel, scale),
        out_shape=(
            jax.ShapeDtypeStruct((width, width), F32),
            jax.ShapeDtypeStruct((width, width), BF16),
            jax.ShapeDtypeStruct((width, width), BF16),
        ),
        in_specs=[vmem],
        out_specs=(vmem, vmem, vmem),
        scratch_shapes=[pltpu.VMEM((width, width), F32)],
        compiler_params=pltpu.CompilerParams(vmem_limit_bytes=48 << 20),
        cost_estimate=pl.CostEstimate(
            flops=width**3, bytes_accessed=12 * width * width, transcendentals=0
        ),
        name="factor",
    )(gram)


def whiten_kernel(x_ref, mean_ref, mh_ref, ml_ref, o_ref):
    width = x_ref.shape[1]
    h, l = split(x_ref[...] - mean_ref[...])
    for j in range(0, width, 2 * B):
        top = j + 2 * B
        mh = mh_ref[j:top, :top]
        ml = ml_ref[j:top, :top]
        o = lax.dot_general(h[:, :top], ml, NT, preferred_element_type=F32)
        o += lax.dot_general(l[:, :top], mh, NT, preferred_element_type=F32)
        o += lax.dot_general(h[:, :top], mh, NT, preferred_element_type=F32)
        o_ref[:, j:top] = o


def whiten(x, mean, mh, ml):
    rows, width = x.shape
    step = rows // 6
    whole = lambda i: (0, 0)
    return pl.pallas_call(
        whiten_kernel,
        grid=(rows // step,),
        out_shape=jax.ShapeDtypeStruct((rows, width), F32),
        in_specs=[
            pl.BlockSpec((step, width), lambda i: (i, 0)),
            pl.BlockSpec((1, width), whole),
            pl.BlockSpec((width, width), whole),
            pl.BlockSpec((width, width), whole),
        ],
        out_specs=pl.BlockSpec((step, width), lambda i: (i, 0)),
        compiler_params=pltpu.CompilerParams(vmem_limit_bytes=48 << 20),
        cost_estimate=pl.CostEstimate(
            flops=2 * rows * width * width, bytes_accessed=8 * rows * width, transcendentals=0
        ),
        name="whiten",
    )(x, mean, mh, ml)


def shards(dims, row_count, embeddings):
    gram, mean = summed_gram(dims, embeddings)
    scale = math.sqrt(row_count)
    r, mh, ml = factor(gram, embeddings.shape[1], scale)
    return whiten(embeddings, mean, mh, ml), r


def solution(mesh):
    nx = mesh.shape["grp"]
    ny = 4
    nz = mesh.shape["wide"] // (2 * ny)

    def whole(embeddings):
        rows, width = embeddings.shape
        return jax.shard_map(
            functools.partial(shards, (nx, ny, nz, width), rows),
            mesh=mesh,
            in_specs=(P(("grp", "wide"), None),),
            out_specs=(P(("grp", "wide"), None), P()),
            check_vma=False,
        )(embeddings)

    return whole
```

```python
import functools
import math

import jax
import jax.numpy as jnp
from jax import lax
from jax.experimental import pallas as pl
from jax.experimental.pallas import tpu as pltpu
from jax.sharding import PartitionSpec as P

F32 = jnp.float32
BF16 = jnp.bfloat16
HI = lax.Precision.HIGHEST
MESH = pl.DeviceIdType.MESH
B = 128
TT = (((0,), (0,)), ((), ()))
NT = (((1,), (1,)), ((), ()))


def tri_blocks(nb):
    return [
        (i, j)
        for pair in range(nb // 2 - 1, -1, -1)
        for j in (2 * pair, 2 * pair + 1)
        for i in range(j + 1)
    ]


def split(x):
    hi = x.astype(BF16)
    return hi, (x - hi.astype(F32)).astype(BF16)


def gram_kernel(
    dims,
    x_hbm,
    out_ref,
    mean_ref,
    xv,
    hi,
    lo,
    own,
    g_ref,
    bmat,
    from_core,
    a_in,
    b_own,
    b_in,
    z_own,
    z_in,
    z_all,
    b_all,
    mbuf,
    m_near,
    m_far,
    dm,
    ssem,
    rsem,
    xsem,
):
    nx, ny, nz, width = dims
    rows = xv.shape[0]
    nb = width // B
    blocks = tri_blocks(nb)
    at = {ij: k for k, ij in enumerate(blocks)}

    chunk = rows // 6
    x_copies = []
    for c in range(6):
        part = slice(c * chunk, (c + 1) * chunk)
        x_copies.append(pltpu.make_async_copy(x_hbm.at[part], xv.at[part], xsem.at[c]))
        x_copies[-1].start()

    mx = lax.axis_index("grp")
    wide = lax.axis_index("wide")
    mc = lax.rem(wide, 2)
    chip = wide // 2
    mz = lax.rem(chip, nz)
    my = chip // nz

    def dev(x, y, z, c):
        return (x, (y * nz + z) * 2 + c)

    def x_peer(d):
        return dev(lax.rem(mx + d, nx), my, mz, mc)

    def y_peer(d):
        return dev(mx, lax.rem(my + d, ny), mz, mc)

    def z_peer(d):
        return dev(mx, my, lax.rem(mz + d, nz), mc)

    core_peer = dev(mx, my, mz, 1 - mc)
    near = (
        [core_peer]
        + [x_peer(d) for d in range(1, nx)]
        + [dev(lax.rem(mx + d, nx), my, mz, 1 - mc) for d in range(1, nx)]
    )
    y_peers = [y_peer(d) for d in range(1, ny)]
    z_peers = [z_peer(d) for d in range(1, nz)]
    everyone = near + y_peers + z_peers
    barrier = pltpu.get_barrier_semaphore()
    for who in everyone:
        pl.semaphore_signal(barrier, inc=1, device_id=who, device_id_type=MESH)

    sent = []

    def send(src, dst, who):
        k = len(sent)
        copy = pltpu.make_async_remote_copy(
            src_ref=src,
            dst_ref=dst,
            send_sem=ssem.at[k],
            recv_sem=rsem.at[k],
            device_id=who,
            device_id_type=MESH,
        )
        copy.start()
        sent.append(copy)
        return copy

    total = jnp.zeros((1, width), F32)
    for c in range(6):
        x_copies[c].wait()
        total = total + jnp.sum(xv[c * chunk : (c + 1) * chunk, :], axis=0, keepdims=True)
    local = total * (1.0 / rows)
    mbuf[...] = jnp.zeros((8, B), F32)
    for i in range(nb):
        mbuf[i : i + 1, :] = local[:, i * B : (i + 1) * B]
    pl.semaphore_wait(barrier, len(everyone))

    slot = mx * 2 + mc
    near_copies = [send(mbuf, m_near.at[slot], who) for who in near]
    m_near[slot] = mbuf[...]

    for c in range(6):
        part = slice(c * chunk, (c + 1) * chunk)
        h, l = split(xv[part, :] - local)
        hi[part, :] = h
        lo[part, :] = l

    own_t = own.reshape(nx, 2, 2, -1, B)
    core_t = from_core.reshape(nx, 2, -1, B)
    ta = own_t.shape[3]
    g_t = g_ref.reshape(nx, 2, 2, ta, B)
    tb = b_in.shape[2]
    tz = z_in.shape[1]

    def near_mean():
        for copy in near_copies:
            copy.wait_recv()
        acc = m_near[0]
        for k in range(1, 2 * nx):
            acc = acc + m_near[k]
        return acc * (1.0 / (2 * nx))

    core_copies = {}
    far_copies = []
    done = 0
    for step in range(nb // 2):
        pair = nb // 2 - 1 - step
        top = 2 * B * (pair + 1)
        cols = slice(2 * B * pair, top)
        g = lax.dot_general(hi[:, :top], hi[:, cols], TT, preferred_element_type=F32)
        g += lax.dot_general(hi[:, :top], lo[:, cols], TT, preferred_element_type=F32)
        g += lax.dot_general(lo[:, :top], hi[:, cols], TT, preferred_element_type=F32)
        g += lax.dot_general(lo[:, :top], lo[:, cols], TT, preferred_element_type=F32)
        if step == 0:
            group = near_mean()
            m_far[mz, my] = group
            y_copies = [send(m_far.at[mz, my], m_far.at[mz, my], who) for who in y_peers]
            delta = mbuf[...] - group
            delta_t = delta.T * float(rows)
            col = [jnp.broadcast_to(delta_t[:, i : i + 1], (B, B)) for i in range(nb)]
        if step == 1:
            for copy in y_copies:
                copy.wait_recv()
            far_copies = [send(m_far.at[mz], m_far.at[mz], who) for who in z_peers]
        for j in (2 * pair, 2 * pair + 1):
            row = jnp.broadcast_to(delta[j : j + 1, :], (B, B))
            for i in range(j + 1):
                off = (j - 2 * pair) * B
                own[at[i, j]] = g[i * B : (i + 1) * B, off : off + B] + col[i] * row
        done += 4 * pair + 3
        for k in range(nx):
            for q in range(2):
                if (k, q) not in core_copies and (4 * k + 2 * q + 2) * ta <= done * B:
                    core_copies[k, q] = send(own_t.at[k, q, 1 - mc], core_t.at[k, q], core_peer)

    ax = [(x_peer, mx), (y_peer, my)]
    a_copies = [[], []]
    for c in core_copies.values():
        c.wait_recv()
    for d in list(range(1, nx)) + [0]:
        for q in range(2):
            peer, me = ax[q]
            k = lax.rem(me + d, nx)
            own_t[k, q, mc] = own_t[k, q, mc] + core_t[k, q]
            if d:
                a_copies[q].append(send(own_t.at[k, q, mc], a_in.at[q, d - 1], peer(d)))
    b_copies = [[], []]
    for q in range(2):
        me = ax[q][1]
        acc = own_t[me, q, mc]
        for d in range(1, nx):
            a_copies[q][d - 1].wait_recv()
            acc = acc + a_in[q, d - 1]
        b_own[q, 0:ta] = acc
        b_own[q, ta:] = jnp.zeros((b_own.shape[1] - ta, B), F32)
        peer, me = ax[1 - q]
        for d in range(1, ny):
            k = lax.rem(me + d, ny)
            b_copies[q].append(
                send(
                    b_own.at[q, pl.ds(pl.multiple_of(k * tb, 8), tb)],
                    b_in.at[q, d - 1],
                    peer(d),
                )
            )
    for q in range(2):
        me = ax[1 - q][1]
        acc = b_own[q, pl.ds(pl.multiple_of(me * tb, 8), tb)]
        for d in range(1, ny):
            b_copies[q][d - 1].wait_recv()
            acc = acc + b_in[q, d - 1]
        z_own[q * tb : (q + 1) * tb] = acc
    z_own[2 * tb :] = jnp.zeros((z_own.shape[0] - 2 * tb, B), F32)
    z_copies = []
    for d in range(1, nz):
        k = lax.rem(mz + d, nz)
        z_copies.append(
            send(z_own.at[pl.ds(pl.multiple_of(k * tz, 8), tz)], z_in.at[d - 1], z_peer(d))
        )

    for copy in far_copies:
        copy.wait_recv()
    m_groups = m_far.reshape(nz * ny, 8, B)
    for i in range(nb):
        rows_i = m_groups[:, i, :]
        mean_i = jnp.sum(rows_i, axis=0, keepdims=True) * (1.0 / (nz * ny))
        mean_ref[:, i * B : (i + 1) * B] = mean_i
        dm[:, i * B : (i + 1) * B] = rows_i - mean_i

    acc = z_own[pl.ds(pl.multiple_of(mz * tz, 8), tz)]
    for d in range(1, nz):
        z_copies[d - 1].wait_recv()
        acc = acc + z_in[d - 1]
    mine = pl.ds(pl.multiple_of(mz * tz, 8), tz)
    z_all[mine] = acc
    z_copies = [send(z_all.at[mine], z_all.at[mine], who) for who in z_peers]

    for pair in range(nb // 2):
        top = 2 * B * (pair + 1)
        g = lax.dot_general(
            dm[:, :top], dm[:, top - 2 * B : top], TT, precision=HI, preferred_element_type=F32
        ) * float(2 * nx * rows)
        for j in (2 * pair, 2 * pair + 1):
            for i in range(j + 1):
                off = (j - 2 * pair) * B
                bmat[at[i, j]] = g[i * B : (i + 1) * B, off : off + B]

    for c in z_copies:
        c.wait_recv()
    b_copies = [[], []]
    for q in range(2):
        peer, me = ax[1 - q]
        mine = pl.ds(pl.multiple_of(me * tb, 8), tb)
        src = z_all.at[q * tb : (q + 1) * tb]
        b_copies[q] = [send(src, b_all.at[q, mine], peer(d)) for d in range(1, ny)]
        b_all[q, mine] = z_all[q * tb : (q + 1) * tb]
    a_copies = [[], []]
    back = []
    for q in range(2):
        for c in b_copies[q]:
            c.wait_recv()
        peer, me = ax[q]
        src = b_all.at[q, 0:ta]
        a_copies[q] = [send(src, g_t.at[me, q, mc], peer(d)) for d in range(1, nx)]
        back.append(send(src, g_t.at[me, q, mc], core_peer))
        g_t[me, q, mc] = b_all[q, 0:ta]
    for d in range(1, nx):
        for q in range(2):
            a_copies[q][d - 1].wait_recv()
            k = lax.rem(ax[q][1] + nx - d, nx)
            back.append(send(g_t.at[k, q, mc], g_t.at[k, q, mc], core_peer))
    for c in back:
        c.wait_recv()
    for k in range(len(blocks)):
        out_ref[k] = g_ref[k] + bmat[k]
    for c in sent:
        c.wait_send()


def summed_gram(dims, x):
    nx, ny, nz, width = dims
    rows = x.shape[0]
    nb = width // B
    n_blocks = nb * (nb + 1) // 2
    total = n_blocks * B
    ta = total // (4 * nx)
    tb = -(-ta // (8 * ny)) * 8
    tz = -(-2 * tb // (8 * nz)) * 8
    n_mean = 2 * nx - 1 + (ny - 1) + (nz - 1)
    n_copies = n_mean + 2 * (2 * nx + 2 * (nx - 1) + 2 * (ny - 1) + nz - 1)
    vmem = pl.BlockSpec(memory_space=pltpu.VMEM)
    return pl.pallas_call(
        functools.partial(gram_kernel, dims),
        out_shape=(
            jax.ShapeDtypeStruct((n_blocks, B, B), F32),
            jax.ShapeDtypeStruct((1, width), F32),
        ),
        in_specs=[pl.BlockSpec(memory_space=pl.ANY)],
        out_specs=(vmem, vmem),
        scratch_shapes=[
            pltpu.VMEM((rows, width), F32),
            pltpu.VMEM((rows, width), BF16),
            pltpu.VMEM((rows, width), BF16),
            pltpu.VMEM((n_blocks, B, B), F32),
            pltpu.VMEM((n_blocks, B, B), F32),
            pltpu.VMEM((n_blocks, B, B), F32),
            pltpu.VMEM((total // 2, B), F32),
            pltpu.VMEM((2, nx - 1, ta, B), F32),
            pltpu.VMEM((2, tb * ny, B), F32),
            pltpu.VMEM((2, ny - 1, tb, B), F32),
            pltpu.VMEM((tz * nz, B), F32),
            pltpu.VMEM((nz - 1, tz, B), F32),
            pltpu.VMEM((tz * nz, B), F32),
            pltpu.VMEM((2, tb * ny, B), F32),
            pltpu.VMEM((8, B), F32),
            pltpu.VMEM((2 * nx, 8, B), F32),
            pltpu.VMEM((nz, ny, 8, B), F32),
            pltpu.VMEM((nz * ny, width), F32),
            pltpu.SemaphoreType.DMA((n_copies,)),
            pltpu.SemaphoreType.DMA((n_copies,)),
            pltpu.SemaphoreType.DMA((6,)),
        ],
        compiler_params=pltpu.CompilerParams(
            collective_id=0, has_side_effects=True, vmem_limit_bytes=56 << 20
        ),
        cost_estimate=pl.CostEstimate(
            flops=2 * rows * width * width, bytes_accessed=4 * rows * width, transcendentals=0
        ),
        name="summed_gram",
    )(x)


def rows_bcast(x, k):
    return jnp.broadcast_to(x[k : k + 1, :], (8, B))
def lane_bcast(x, c):
    return jnp.broadcast_to(x[:, c : c + 1], (8, B))


def factor_block(S, ones):
    lane = lax.broadcasted_iota(jnp.int32, (8, B), 1)
    sub = lax.broadcasted_iota(jnp.int32, (8, B), 0)
    S = list(S)
    out = []
    D = [lane_bcast(S[0], l) * ones for l in range(8)]
    for p in range(16):
        base = 8 * p
        inpanel = (lane >= base) & (lane < base + 8)
        C = D
        more = p < 15
        row_s = S[p]
        row_t = jnp.where(inpanel, jnp.where(lane == base + sub, 1.0, 0.0), S[p])
        if more:
            c = [lane_bcast(S[p + 1], base + j) * ones for j in range(8)]
            D = [lane_bcast(S[p + 1], base + 8 + l) * ones for l in range(8)]
            nxt = jnp.where(inpanel, 0.0, S[p + 1])
        pivot = rows_bcast(C[0], 0)
        diag = rdiag = None
        for j in range(8):
            r = 1.0 / pivot
            U = {l: rows_bcast(C[l], j) for l in range(j + 1, 8)}
            m = jnp.where(sub > j, C[j], 0.0) * r
            diag = pivot if j == 0 else jnp.where(sub == j, pivot, diag)
            rdiag = r if j == 0 else jnp.where(sub == j, r, rdiag)
            if j < 7:
                pivot = rows_bcast(C[j + 1], j + 1) - (U[j + 1] * U[j + 1]) * r
            for l in range(j + 1, 8):
                C[l] = C[l] - m * U[l]
            us = rows_bcast(row_s, j)
            ut = rows_bcast(row_t, j)
            row_s = row_s - m * us
            row_t = row_t - m * ut
            if more:
                e = c[j] * r
                for k in range(j + 1, 8):
                    c[k] = c[k] - e * U[k]
                for l in range(8):
                    D[l] = D[l] - e * rows_bcast(c[j], l)
                nxt = nxt - e * ut
        rs = lax.rsqrt(diag)
        out.append(jnp.where(lane > base + sub, row_s, row_t) * rs)
        if p < 14:
            Q = row_t * rdiag
            for l in range(7, 0, -1):
                Q = Q - (jnp.where(sub < l, C[l], 0.0) * rdiag) * rows_bcast(Q, l)
            q = [rows_bcast(Q, j) for j in range(8)]
            for i in range(p + 2, 16):
                acc = jnp.where(inpanel, 0.0, S[i])
                for j in range(8):
                    acc = acc - lane_bcast(S[i], base + j) * q[j]
                S[i] = acc
        if more:
            S[p + 1] = nxt
    return out

def factor_whiten_kernel(scale, g_ref, mean_ref, x_hbm, r_ref, o_hbm, w_ref, mh, ml, xv, hi, lo, o, xsem, osem, ones_ref):
    n = r_ref.shape[0]
    nb = n // B
    rows = xv.shape[0]
    CH = rows // 4
    xcopies = [pltpu.make_async_copy(x_hbm.at[c*CH:(c+1)*CH], xv.at[c*CH:(c+1)*CH], xsem.at[c]) for c in range(4)]
    for c in xcopies: c.start()
    for k, (i, j) in enumerate(tri_blocks(nb)):
        w_ref[i * B : (i + 1) * B, j * B : (j + 1) * B] = g_ref[k]
    li = lax.broadcasted_iota(jnp.int32, (B, B), 0)
    lj = lax.broadcasted_iota(jnp.int32, (B, B), 1)
    inv = 1.0 / scale

    def dot(a, b):
        return jnp.dot(a, b, precision=HI, preferred_element_type=F32)

    def dot_t(a, b):
        return lax.dot_general(a, b, TT, precision=HI, preferred_element_type=F32)

    def do_split(c):
        def f():
            if c % 4 == 0: xcopies[c // 4].wait()
            s = slice(c * CH // 4, (c + 1) * CH // 4)
            h, l = split(xv[s, :] - mean_ref[...])
            hi[s, :] = h
            lo[s, :] = l
        return f

    def do_whiten(b, c):
        def f():
            s = slice(c * CH, (c + 1) * CH)
            cs = slice(B * b, B * (b + 1))
            top = B * (b + 1)
            h = hi[s, :top]
            a = lax.dot_general(h, ml[cs, :top], NT, preferred_element_type=F32)
            a += lax.dot_general(lo[s, :top], mh[cs, :top], NT, preferred_element_type=F32)
            a += lax.dot_general(h, mh[cs, :top], NT, preferred_element_type=F32)
            o[s, cs] = a
        return f

    ocopies = []
    def out_copy(b):
        def f():
            cs = slice(B * b, B * (b + 1))
            cp = pltpu.make_async_copy(o.at[:, cs], o_hbm.at[:, cs], osem.at[b])
            cp.start()
            ocopies.append(cp)
        return f

    ones_ref[...] = jnp.full((8, B), 1.0, F32)
    ones = ones_ref[...]
    work = [do_split(c) for c in range(16)]
    for b in range(nb):
        bs = slice(B * b, B * (b + 1))
        S = [w_ref[B * b + 8 * i : B * b + 8 * i + 8, bs] for i in range(16)]
        for i, t in enumerate(factor_block(S, ones)):
            w_ref[B * b + 8 * i : B * b + 8 * i + 8, bs] = t
        for f in work:
            f()
        F = w_ref[bs, bs]
        M = jnp.where(li >= lj, F, 0.0)
        before = slice(0, B * b)
        after = slice(B * (b + 1), n)
        nxt = slice(B * (b + 1), B * (b + 2))
        beyond = slice(B * (b + 2), n)
        if b < nb - 1:
            Rn = dot(M, w_ref[bs, nxt])
            w_ref[bs, nxt] = Rn
            w_ref[nxt, nxt] = w_ref[nxt, nxt] - dot_t(Rn, Rn)
        work = []

        def finish_row(b=b, bs=bs, before=before, beyond=beyond, after=after, M=M, F=F):
            if b > 0:
                w_ref[bs, before] = dot(M, w_ref[bs, before])
            if b < nb - 2:
                w_ref[bs, beyond] = dot(M, w_ref[bs, beyond])

        def outputs(b=b, bs=bs, before=before, after=after, M=M, F=F):
            R = jnp.where(li < lj, F, jnp.where(li == lj, 1.0 / F, 0.0))
            r_ref[bs, bs] = R * inv
            h, l = split(M * scale)
            mh[bs, bs] = h
            ml[bs, bs] = l
            if b > 0:
                r_ref[bs, before] = jnp.zeros((B, B * b), F32)
                h, l = split(w_ref[bs, before] * scale)
                mh[bs, before] = h
                ml[bs, before] = l
            if b < nb - 1:
                r_ref[bs, after] = w_ref[bs, after] * inv

        def update_next(b=b, bs=bs, nxt=nxt, before=before, beyond=beyond, M=M):
            Rn = w_ref[bs, nxt]
            if b < nb - 2:
                w_ref[nxt, beyond] = w_ref[nxt, beyond] - dot_t(Rn, w_ref[bs, beyond])
            if b > 0:
                w_ref[nxt, before] = w_ref[nxt, before] - dot_t(Rn, w_ref[bs, before])
            w_ref[nxt, bs] = -dot_t(Rn, M)

        def update_beyond(b=b, bs=bs, before=before, beyond=beyond, M=M):
            Ra = w_ref[bs, beyond]
            w_ref[beyond, beyond] = w_ref[beyond, beyond] - dot_t(Ra, Ra)
            if b > 0:
                w_ref[beyond, before] = w_ref[beyond, before] - dot_t(Ra, w_ref[bs, before])
            w_ref[beyond, bs] = -dot_t(Ra, M)

        work.append(finish_row)
        work.append(outputs)
        if b < nb - 1:
            work.append(update_next)
        if b < nb - 2:
            work.append(update_beyond)
        work += [do_whiten(b, c) for c in range(4)]
        work.append(out_copy(b))
    for f in work:
        f()
    for c in ocopies:
        c.wait()

def factor_whiten(gram, mean, x, scale):
    rows, width = x.shape
    vmem = pl.BlockSpec(memory_space=pltpu.VMEM)
    hbm = pl.BlockSpec(memory_space=pl.ANY)
    return pl.pallas_call(
        functools.partial(factor_whiten_kernel, scale),
        out_shape=(
            jax.ShapeDtypeStruct((width, width), F32),
            jax.ShapeDtypeStruct((rows, width), F32),
        ),
        in_specs=[vmem, vmem, hbm],
        out_specs=(vmem, hbm),
        scratch_shapes=[pltpu.VMEM((width, width), F32), pltpu.VMEM((width, width), BF16), pltpu.VMEM((width, width), BF16),
            pltpu.VMEM((rows, width), F32), pltpu.VMEM((rows, width), BF16), pltpu.VMEM((rows, width), BF16), pltpu.VMEM((rows, width), F32),
            pltpu.SemaphoreType.DMA((4,)), pltpu.SemaphoreType.DMA((width // B,)), pltpu.VMEM((8, B), F32)],
        compiler_params=pltpu.CompilerParams(vmem_limit_bytes=56 << 20),
        name="factor_whiten",
    )(gram, mean, x)


def shards(dims, row_count, embeddings):
    gram, mean = summed_gram(dims, embeddings)
    r, whitened = factor_whiten(gram, mean, embeddings, math.sqrt(row_count))
    return whitened, r


def solution(mesh):
    nx = mesh.shape["grp"]
    ny = 4
    nz = mesh.shape["wide"] // (2 * ny)

    def whole(embeddings):
        rows, width = embeddings.shape
        return jax.shard_map(
            functools.partial(shards, (nx, ny, nz, width), rows),
            mesh=mesh,
            in_specs=(P(("grp", "wide"), None),),
            out_specs=(P(("grp", "wide"), None), P()),
            check_vma=False,
        )(embeddings)

    return whole
```

```python
import functools
import math

import jax
import jax.numpy as jnp
from jax import lax
from jax.experimental import pallas as pl
from jax.experimental.pallas import tpu as pltpu
from jax.sharding import PartitionSpec as P

F32 = jnp.float32
BF16 = jnp.bfloat16
HI = lax.Precision.HIGHEST
MESH = pl.DeviceIdType.MESH
B = 128
TT = (((0,), (0,)), ((), ()))
NT = (((1,), (1,)), ((), ()))


def row_pairs(nb):
    return [
        [(i, j) for i in (2 * pair, 2 * pair + 1) for j in range(i, nb)]
        for pair in range(nb // 2)
    ]


def tri_blocks(nb):
    return [ij for pair in row_pairs(nb) for ij in pair]


def split(x):
    hi = x.astype(BF16)
    return hi, (x - hi.astype(F32)).astype(BF16)


def gram_kernel(
    dims,
    x_hbm,
    out_ref,
    mean_ref,
    xv,
    hi,
    lo,
    own0,
    own1,
    own2,
    core0,
    core1,
    core2,
    a_in0,
    a_in1,
    a_in2,
    head,
    tail,
    bmat,
    b_own,
    b_in,
    z_own,
    z_in,
    z_all,
    b_all,
    mbuf,
    m_near,
    m_far,
    dm,
    ssem,
    rsem,
    xsem,
):
    nx, ny, nz, width = dims
    rows = xv.shape[0]
    nb = width // B
    blocks = tri_blocks(nb)
    at = {ij: k for k, ij in enumerate(blocks)}

    chunk = rows // 6
    x_copies = []
    for c in range(6):
        part = slice(c * chunk, (c + 1) * chunk)
        x_copies.append(pltpu.make_async_copy(x_hbm.at[part], xv.at[part], xsem.at[c]))
        x_copies[-1].start()

    mx = lax.axis_index("grp")
    wide = lax.axis_index("wide")
    mc = lax.rem(wide, 2)
    chip = wide // 2
    mz = lax.rem(chip, nz)
    my = chip // nz

    def dev(x, y, z, c):
        return (x, (y * nz + z) * 2 + c)

    def x_peer(d):
        return dev(lax.rem(mx + d, nx), my, mz, mc)

    def y_peer(d):
        return dev(mx, lax.rem(my + d, ny), mz, mc)

    def z_peer(d):
        return dev(mx, my, lax.rem(mz + d, nz), mc)

    core_peer = dev(mx, my, mz, 1 - mc)
    near = (
        [core_peer]
        + [x_peer(d) for d in range(1, nx)]
        + [dev(lax.rem(mx + d, nx), my, mz, 1 - mc) for d in range(1, nx)]
    )
    y_peers = [y_peer(d) for d in range(1, ny)]
    z_peers = [z_peer(d) for d in range(1, nz)]
    everyone = near + y_peers + z_peers
    barrier = pltpu.get_barrier_semaphore()
    for who in everyone:
        pl.semaphore_signal(barrier, inc=1, device_id=who, device_id_type=MESH)

    sent = []

    def send(src, dst, who):
        k = len(sent)
        copy = pltpu.make_async_remote_copy(
            src_ref=src,
            dst_ref=dst,
            send_sem=ssem.at[k],
            recv_sem=rsem.at[k],
            device_id=who,
            device_id_type=MESH,
        )
        copy.start()
        sent.append(copy)
        return copy

    total = jnp.zeros((1, width), F32)
    for c in range(6):
        x_copies[c].wait()
        total = total + jnp.sum(xv[c * chunk : (c + 1) * chunk, :], axis=0, keepdims=True)
    local = total * (1.0 / rows)
    mbuf[...] = jnp.zeros((8, B), F32)
    for i in range(nb):
        mbuf[i : i + 1, :] = local[:, i * B : (i + 1) * B]
    pl.semaphore_wait(barrier, len(everyone))

    slot = mx * 2 + mc
    near_copies = [send(mbuf, m_near.at[slot], who) for who in near]
    m_near[slot] = mbuf[...]

    for c in range(6):
        part = slice(c * chunk, (c + 1) * chunk)
        h, l = split(xv[part, :] - local)
        hi[part, :] = h
        lo[part, :] = l

    pairs = row_pairs(nb)
    own = (own0, own1, own2)
    core_in = (core0, core1, core2)
    a_in = (a_in0, a_in1, a_in2)
    part = [a.shape[2] for a in a_in]
    first = [sum(part[:k]) for k in range(len(part))]
    own_t = [o.reshape(2, 2, nx, n, B) for o, n in zip(own, part)]
    ta = sum(part)
    tb = b_in.shape[2]
    tz = z_in.shape[1]
    ax = [(x_peer, mx), (y_peer, my)]

    def near_mean():
        for copy in near_copies:
            copy.wait_recv()
        acc = m_near[0]
        for k in range(1, 2 * nx):
            acc = acc + m_near[k]
        return acc * (1.0 / (2 * nx))

    core_copies = []
    a_copies = []

    def scatter_a(k):
        core_copies[k].wait_recv()
        own_t[k][mc] = own_t[k][mc] + core_in[k][...]
        copies = [[], []]
        for d in range(1, nx):
            for q in range(2):
                peer, me = ax[q]
                to = lax.rem(me + d, nx)
                copies[q].append(send(own_t[k].at[mc, q, to], a_in[k].at[q, d - 1], peer(d)))
        a_copies.append(copies)

    for k, pair in enumerate(pairs):
        rs = slice(2 * B * k, 2 * B * (k + 1))
        rest = slice(2 * B * k, width)
        g = lax.dot_general(hi[:, rs], hi[:, rest], TT, preferred_element_type=F32)
        g += lax.dot_general(hi[:, rs], lo[:, rest], TT, preferred_element_type=F32)
        g += lax.dot_general(lo[:, rs], hi[:, rest], TT, preferred_element_type=F32)
        if k == 0:
            group = near_mean()
            m_far[mz, my] = group
            y_copies = [send(m_far.at[mz, my], m_far.at[mz, my], who) for who in y_peers]
            delta = mbuf[...] - group
            delta_t = delta.T * float(rows)
        for n, (i, j) in enumerate(pair):
            col = jnp.broadcast_to(delta_t[:, i : i + 1], (B, B))
            row = jnp.broadcast_to(delta[j : j + 1, :], (B, B))
            gi, gj = (i - 2 * k) * B, (j - 2 * k) * B
            own[k][n] = g[gi : gi + B, gj : gj + B] + col * row
        core_copies.append(send(own_t[k].at[1 - mc], core_in[k], core_peer))
        if k:
            scatter_a(k - 1)
    for copy in y_copies:
        copy.wait_recv()
    far_copies = [send(m_far.at[mz], m_far.at[mz], who) for who in z_peers]
    scatter_a(len(pairs) - 1)

    b_copies = [[], []]
    for q in range(2):
        me = ax[q][1]
        for k in range(len(pairs)):
            acc = own_t[k][mc, q, me]
            for d in range(1, nx):
                a_copies[k][q][d - 1].wait_recv()
                acc = acc + a_in[k][q, d - 1]
            b_own[q, first[k] : first[k] + part[k]] = acc
        b_own[q, ta:] = jnp.zeros((b_own.shape[1] - ta, B), F32)
        peer, me = ax[1 - q]
        for d in range(1, ny):
            k = lax.rem(me + d, ny)
            b_copies[q].append(
                send(
                    b_own.at[q, pl.ds(pl.multiple_of(k * tb, 8), tb)],
                    b_in.at[q, d - 1],
                    peer(d),
                )
            )
    for q in range(2):
        me = ax[1 - q][1]
        acc = b_own[q, pl.ds(pl.multiple_of(me * tb, 8), tb)]
        for d in range(1, ny):
            b_copies[q][d - 1].wait_recv()
            acc = acc + b_in[q, d - 1]
        z_own[q * tb : (q + 1) * tb] = acc
    z_own[2 * tb :] = jnp.zeros((z_own.shape[0] - 2 * tb, B), F32)
    z_copies = []
    for d in range(1, nz):
        k = lax.rem(mz + d, nz)
        z_copies.append(
            send(z_own.at[pl.ds(pl.multiple_of(k * tz, 8), tz)], z_in.at[d - 1], z_peer(d))
        )

    for copy in far_copies:
        copy.wait_recv()
    m_groups = m_far.reshape(nz * ny, 8, B)
    for i in range(nb):
        rows_i = m_groups[:, i, :]
        mean_i = jnp.sum(rows_i, axis=0, keepdims=True) * (1.0 / (nz * ny))
        mean_ref[:, i * B : (i + 1) * B] = mean_i
        dm[:, i * B : (i + 1) * B] = rows_i - mean_i

    acc = z_own[pl.ds(pl.multiple_of(mz * tz, 8), tz)]
    for d in range(1, nz):
        z_copies[d - 1].wait_recv()
        acc = acc + z_in[d - 1]
    mine = pl.ds(pl.multiple_of(mz * tz, 8), tz)
    z_all[mine] = acc
    z_copies = [send(z_all.at[mine], z_all.at[mine], who) for who in z_peers]

    for k, pair in enumerate(pairs):
        rs = slice(2 * B * k, 2 * B * (k + 1))
        rest = slice(2 * B * k, width)
        g = lax.dot_general(
            dm[:, rs], dm[:, rest], TT, precision=HI, preferred_element_type=F32
        ) * float(2 * nx * rows)
        for i, j in pair:
            gi, gj = (i - 2 * k) * B, (j - 2 * k) * B
            bmat[at[i, j]] = g[gi : gi + B, gj : gj + B]

    for c in z_copies:
        c.wait_recv()
    b_copies = [[], []]
    for q in range(2):
        peer, me = ax[1 - q]
        mine = pl.ds(pl.multiple_of(me * tb, 8), tb)
        src = z_all.at[q * tb : (q + 1) * tb]
        b_copies[q] = [send(src, b_all.at[q, mine], peer(d)) for d in range(1, ny)]
        b_all[q, mine] = z_all[q * tb : (q + 1) * tb]
    back = []
    gathers = []
    for dst, at_row, n in ((head, 0, part[0]), (tail, part[0], ta - part[0])):
        copies = [[], []]
        for q in range(2):
            if dst is head:
                for c in b_copies[q]:
                    c.wait_recv()
            peer, me = ax[q]
            src = b_all.at[q, at_row : at_row + n]
            copies[q] = [send(src, dst.at[mc, q, me], peer(d)) for d in range(1, nx)]
            back.append(send(src, dst.at[mc, q, me], core_peer))
            dst[mc, q, me] = b_all[q, at_row : at_row + n]
        gathers.append(copies)
    for dst, copies in zip((head, tail), gathers):
        for d in range(1, nx):
            for q in range(2):
                copies[q][d - 1].wait_recv()
                k = lax.rem(ax[q][1] + nx - d, nx)
                back.append(send(dst.at[mc, q, k], dst.at[mc, q, k], core_peer))
    for c in back:
        c.wait_recv()
    n_head = len(pairs[0])
    whole_head = head.reshape(n_head, B, B)
    for k in range(n_head):
        out_ref[k] = whole_head[k] + bmat[k]
    pieces = tail.reshape(4 * nx, ta - part[0], B)
    start = n_head
    for k in range(1, len(pairs)):
        for t in range(len(pairs[k]) * B // 8):
            piece, off = divmod(8 * t, part[k])
            off += first[k] - part[0]
            block, row = start + 8 * t // B, 8 * t % B
            out_ref[block, row : row + 8] = (
                pieces[piece, off : off + 8] + bmat[block, row : row + 8]
            )
        start += len(pairs[k])
    for c in sent:
        c.wait_send()


def summed_gram(dims, x):
    nx, ny, nz, width = dims
    rows = x.shape[0]
    nb = width // B
    n_blocks = nb * (nb + 1) // 2
    sizes = [len(pair) for pair in row_pairs(nb)]
    part = [n * B // (4 * nx) for n in sizes]
    ta = sum(part)
    tb = -(-ta // (8 * ny)) * 8
    tz = -(-2 * tb // (8 * nz)) * 8
    n_mean = 2 * nx - 1 + (ny - 1) + (nz - 1)
    n_copies = n_mean + 3 + 6 * (nx - 1) + 4 * (ny - 1) + 2 * (nz - 1) + 4 * (nx - 1) + 4 * nx
    vmem = pl.BlockSpec(memory_space=pltpu.VMEM)
    return pl.pallas_call(
        functools.partial(gram_kernel, dims),
        out_shape=(
            jax.ShapeDtypeStruct((n_blocks, B, B), F32),
            jax.ShapeDtypeStruct((1, width), F32),
        ),
        in_specs=[pl.BlockSpec(memory_space=pl.ANY)],
        out_specs=(vmem, vmem),
        scratch_shapes=[
            pltpu.VMEM((rows, width), F32),
            pltpu.VMEM((rows, width), BF16),
            pltpu.VMEM((rows, width), BF16),
            *[pltpu.VMEM((n, B, B), F32) for n in sizes],
            *[pltpu.VMEM((2, nx, n, B), F32) for n in part],
            *[pltpu.VMEM((2, nx - 1, n, B), F32) for n in part],
            pltpu.VMEM((2, 2, nx, part[0], B), F32),
            pltpu.VMEM((2, 2, nx, ta - part[0], B), F32),
            pltpu.VMEM((n_blocks, B, B), F32),
            pltpu.VMEM((2, tb * ny, B), F32),
            pltpu.VMEM((2, ny - 1, tb, B), F32),
            pltpu.VMEM((tz * nz, B), F32),
            pltpu.VMEM((nz - 1, tz, B), F32),
            pltpu.VMEM((tz * nz, B), F32),
            pltpu.VMEM((2, tb * ny, B), F32),
            pltpu.VMEM((8, B), F32),
            pltpu.VMEM((2 * nx, 8, B), F32),
            pltpu.VMEM((nz, ny, 8, B), F32),
            pltpu.VMEM((nz * ny, width), F32),
            pltpu.SemaphoreType.DMA((n_copies,)),
            pltpu.SemaphoreType.DMA((n_copies,)),
            pltpu.SemaphoreType.DMA((6,)),
        ],
        compiler_params=pltpu.CompilerParams(
            collective_id=0, has_side_effects=True, vmem_limit_bytes=56 << 20
        ),
        cost_estimate=pl.CostEstimate(
            flops=2 * rows * width * width, bytes_accessed=4 * rows * width, transcendentals=0
        ),
        name="summed_gram",
    )(x)


def rows_bcast(x, k):
    return jnp.broadcast_to(x[k : k + 1, :], (8, B))
def lane_bcast(x, c):
    return jnp.broadcast_to(x[:, c : c + 1], (8, B))


def factor_block(S, ones):
    lane = lax.broadcasted_iota(jnp.int32, (8, B), 1)
    sub = lax.broadcasted_iota(jnp.int32, (8, B), 0)
    S = list(S)
    out = []
    D = [lane_bcast(S[0], l) * ones for l in range(8)]
    for p in range(16):
        base = 8 * p
        inpanel = (lane >= base) & (lane < base + 8)
        C = D
        more = p < 15
        row_s = S[p]
        row_t = jnp.where(inpanel, jnp.where(lane == base + sub, 1.0, 0.0), S[p])
        if more:
            c = [lane_bcast(S[p + 1], base + j) * ones for j in range(8)]
            D = [lane_bcast(S[p + 1], base + 8 + l) * ones for l in range(8)]
            nxt = jnp.where(inpanel, 0.0, S[p + 1])
        pivot = rows_bcast(C[0], 0)
        diag = rdiag = None
        for j in range(8):
            r = 1.0 / pivot
            U = {l: rows_bcast(C[l], j) for l in range(j + 1, 8)}
            m = jnp.where(sub > j, C[j], 0.0) * r
            diag = pivot if j == 0 else jnp.where(sub == j, pivot, diag)
            rdiag = r if j == 0 else jnp.where(sub == j, r, rdiag)
            if j < 7:
                pivot = rows_bcast(C[j + 1], j + 1) - (U[j + 1] * U[j + 1]) * r
            for l in range(j + 1, 8):
                C[l] = C[l] - m * U[l]
            us = rows_bcast(row_s, j)
            ut = rows_bcast(row_t, j)
            row_s = row_s - m * us
            row_t = row_t - m * ut
            if more:
                e = c[j] * r
                for k in range(j + 1, 8):
                    c[k] = c[k] - e * U[k]
                for l in range(8):
                    D[l] = D[l] - e * rows_bcast(c[j], l)
                nxt = nxt - e * ut
        rs = lax.rsqrt(diag)
        out.append(jnp.where(lane > base + sub, row_s, row_t) * rs)
        if p < 14:
            Q = row_t * rdiag
            for l in range(7, 0, -1):
                Q = Q - (jnp.where(sub < l, C[l], 0.0) * rdiag) * rows_bcast(Q, l)
            q = [rows_bcast(Q, j) for j in range(8)]
            for i in range(p + 2, 16):
                acc = jnp.where(inpanel, 0.0, S[i])
                for j in range(8):
                    acc = acc - lane_bcast(S[i], base + j) * q[j]
                S[i] = acc
        if more:
            S[p + 1] = nxt
    return out

def factor_whiten_kernel(scale, g_ref, mean_ref, x_hbm, r_ref, o_hbm, w_ref, mh, ml, xv, hi, lo, o, xsem, osem, ones_ref):
    n = r_ref.shape[0]
    nb = n // B
    rows = xv.shape[0]
    CH = rows // 4
    xcopies = [pltpu.make_async_copy(x_hbm.at[c*CH:(c+1)*CH], xv.at[c*CH:(c+1)*CH], xsem.at[c]) for c in range(4)]
    for c in xcopies: c.start()
    for k, (i, j) in enumerate(tri_blocks(nb)):
        w_ref[i * B : (i + 1) * B, j * B : (j + 1) * B] = g_ref[k]
    li = lax.broadcasted_iota(jnp.int32, (B, B), 0)
    lj = lax.broadcasted_iota(jnp.int32, (B, B), 1)
    inv = 1.0 / scale

    def dot(a, b):
        return jnp.dot(a, b, precision=HI, preferred_element_type=F32)

    def dot_t(a, b):
        return lax.dot_general(a, b, TT, precision=HI, preferred_element_type=F32)

    def do_split(c):
        def f():
            if c % 4 == 0: xcopies[c // 4].wait()
            s = slice(c * CH // 4, (c + 1) * CH // 4)
            h, l = split(xv[s, :] - mean_ref[...])
            hi[s, :] = h
            lo[s, :] = l
        return f

    def do_whiten(b, c):
        def f():
            s = slice(c * CH, (c + 1) * CH)
            cs = slice(B * b, B * (b + 1))
            top = B * (b + 1)
            h = hi[s, :top]
            a = lax.dot_general(h, ml[cs, :top], NT, preferred_element_type=F32)
            a += lax.dot_general(lo[s, :top], mh[cs, :top], NT, preferred_element_type=F32)
            a += lax.dot_general(h, mh[cs, :top], NT, preferred_element_type=F32)
            o[s, cs] = a
        return f

    ocopies = []
    def out_copy(b):
        def f():
            cs = slice(B * b, B * (b + 1))
            cp = pltpu.make_async_copy(o.at[:, cs], o_hbm.at[:, cs], osem.at[b])
            cp.start()
            ocopies.append(cp)
        return f

    ones_ref[...] = jnp.full((8, B), 1.0, F32)
    ones = ones_ref[...]
    work = [do_split(c) for c in range(16)]
    for b in range(nb):
        bs = slice(B * b, B * (b + 1))
        S = [w_ref[B * b + 8 * i : B * b + 8 * i + 8, bs] for i in range(16)]
        for i, t in enumerate(factor_block(S, ones)):
            w_ref[B * b + 8 * i : B * b + 8 * i + 8, bs] = t
        for f in work:
            f()
        F = w_ref[bs, bs]
        M = jnp.where(li >= lj, F, 0.0)
        before = slice(0, B * b)
        after = slice(B * (b + 1), n)
        nxt = slice(B * (b + 1), B * (b + 2))
        beyond = slice(B * (b + 2), n)
        if b < nb - 1:
            Rn = dot(M, w_ref[bs, nxt])
            w_ref[bs, nxt] = Rn
            w_ref[nxt, nxt] = w_ref[nxt, nxt] - dot_t(Rn, Rn)
        work = []

        def finish_row(b=b, bs=bs, before=before, beyond=beyond, after=after, M=M, F=F):
            if b > 0:
                w_ref[bs, before] = dot(M, w_ref[bs, before])
            if b < nb - 2:
                w_ref[bs, beyond] = dot(M, w_ref[bs, beyond])

        def outputs(b=b, bs=bs, before=before, after=after, M=M, F=F):
            R = jnp.where(li < lj, F, jnp.where(li == lj, 1.0 / F, 0.0))
            r_ref[bs, bs] = R * inv
            h, l = split(M * scale)
            mh[bs, bs] = h
            ml[bs, bs] = l
            if b > 0:
                r_ref[bs, before] = jnp.zeros((B, B * b), F32)
                h, l = split(w_ref[bs, before] * scale)
                mh[bs, before] = h
                ml[bs, before] = l
            if b < nb - 1:
                r_ref[bs, after] = w_ref[bs, after] * inv

        def update_next(b=b, bs=bs, nxt=nxt, before=before, beyond=beyond, M=M):
            Rn = w_ref[bs, nxt]
            if b < nb - 2:
                w_ref[nxt, beyond] = w_ref[nxt, beyond] - dot_t(Rn, w_ref[bs, beyond])
            if b > 0:
                w_ref[nxt, before] = w_ref[nxt, before] - dot_t(Rn, w_ref[bs, before])
            w_ref[nxt, bs] = -dot_t(Rn, M)

        def update_beyond(b=b, bs=bs, before=before, beyond=beyond, M=M):
            Ra = w_ref[bs, beyond]
            w_ref[beyond, beyond] = w_ref[beyond, beyond] - dot_t(Ra, Ra)
            if b > 0:
                w_ref[beyond, before] = w_ref[beyond, before] - dot_t(Ra, w_ref[bs, before])
            w_ref[beyond, bs] = -dot_t(Ra, M)

        work.append(finish_row)
        work.append(outputs)
        if b < nb - 1:
            work.append(update_next)
        if b < nb - 2:
            work.append(update_beyond)
        work += [do_whiten(b, c) for c in range(4)]
        work.append(out_copy(b))
    for f in work:
        f()
    for c in ocopies:
        c.wait()

def factor_whiten(gram, mean, x, scale):
    rows, width = x.shape
    vmem = pl.BlockSpec(memory_space=pltpu.VMEM)
    hbm = pl.BlockSpec(memory_space=pl.ANY)
    return pl.pallas_call(
        functools.partial(factor_whiten_kernel, scale),
        out_shape=(
            jax.ShapeDtypeStruct((width, width), F32),
            jax.ShapeDtypeStruct((rows, width), F32),
        ),
        in_specs=[vmem, vmem, hbm],
        out_specs=(vmem, hbm),
        scratch_shapes=[pltpu.VMEM((width, width), F32), pltpu.VMEM((width, width), BF16), pltpu.VMEM((width, width), BF16),
            pltpu.VMEM((rows, width), F32), pltpu.VMEM((rows, width), BF16), pltpu.VMEM((rows, width), BF16), pltpu.VMEM((rows, width), F32),
            pltpu.SemaphoreType.DMA((4,)), pltpu.SemaphoreType.DMA((width // B,)), pltpu.VMEM((8, B), F32)],
        compiler_params=pltpu.CompilerParams(vmem_limit_bytes=56 << 20),
        name="factor_whiten",
    )(gram, mean, x)


def shards(dims, row_count, embeddings):
    gram, mean = summed_gram(dims, embeddings)
    r, whitened = factor_whiten(gram, mean, embeddings, math.sqrt(row_count))
    return whitened, r


def solution(mesh):
    nx = mesh.shape["grp"]
    ny = 4
    nz = mesh.shape["wide"] // (2 * ny)

    def whole(embeddings):
        rows, width = embeddings.shape
        return jax.shard_map(
            functools.partial(shards, (nx, ny, nz, width), rows),
            mesh=mesh,
            in_specs=(P(("grp", "wide"), None),),
            out_specs=(P(("grp", "wide"), None), P()),
            check_vma=False,
        )(embeddings)

    return whole
```

```python
import functools
import math

import jax
import jax.numpy as jnp
from jax import lax
from jax.experimental import pallas as pl
from jax.experimental.pallas import tpu as pltpu
from jax.sharding import PartitionSpec as P

F32 = jnp.float32
BF16 = jnp.bfloat16
HI = lax.Precision.HIGHEST
MESH = pl.DeviceIdType.MESH
B = 128
TT = (((0,), (0,)), ((), ()))
NT = (((1,), (1,)), ((), ()))


def row_pairs(nb):
    return [
        [(i, j) for i in (2 * pair, 2 * pair + 1) for j in range(i, nb)]
        for pair in range(nb // 2)
    ]


def tri_blocks(nb):
    return [ij for pair in row_pairs(nb) for ij in pair]


def split(x):
    hi = x.astype(BF16)
    return hi, (x - hi.astype(F32)).astype(BF16)


def gram_kernel(
    dims,
    x_hbm,
    out_ref,
    mean_ref,
    xv,
    hi,
    lo,
    own0,
    own1,
    own2,
    core0,
    core1,
    core2,
    a_in0,
    a_in1,
    a_in2,
    head,
    tail,
    bmat,
    b_own,
    b_in,
    z_own,
    z_in,
    z_all,
    b_all,
    mbuf,
    m_near,
    m_far,
    dm,
    ssem,
    rsem,
    xsem,
):
    nx, ny, nz, width = dims
    rows = xv.shape[0]
    nb = width // B
    blocks = tri_blocks(nb)
    at = {ij: k for k, ij in enumerate(blocks)}

    chunk = rows // 6
    x_copies = []
    for c in range(6):
        part = slice(c * chunk, (c + 1) * chunk)
        x_copies.append(pltpu.make_async_copy(x_hbm.at[part], xv.at[part], xsem.at[c]))
        x_copies[-1].start()

    mx = lax.axis_index("grp")
    wide = lax.axis_index("wide")
    mc = lax.rem(wide, 2)
    chip = wide // 2
    mz = lax.rem(chip, nz)
    my = chip // nz

    def dev(x, y, z, c):
        return (x, (y * nz + z) * 2 + c)

    def x_peer(d):
        return dev(lax.rem(mx + d, nx), my, mz, mc)

    def y_peer(d):
        return dev(mx, lax.rem(my + d, ny), mz, mc)

    def z_peer(d):
        return dev(mx, my, lax.rem(mz + d, nz), mc)

    core_peer = dev(mx, my, mz, 1 - mc)
    near = (
        [core_peer]
        + [x_peer(d) for d in range(1, nx)]
        + [dev(lax.rem(mx + d, nx), my, mz, 1 - mc) for d in range(1, nx)]
    )
    y_peers = [y_peer(d) for d in range(1, ny)]
    z_peers = [z_peer(d) for d in range(1, nz)]
    everyone = near + y_peers + z_peers
    barrier = pltpu.get_barrier_semaphore()
    for who in everyone:
        pl.semaphore_signal(barrier, inc=1, device_id=who, device_id_type=MESH)

    sent = []

    def send(src, dst, who):
        k = len(sent)
        copy = pltpu.make_async_remote_copy(
            src_ref=src,
            dst_ref=dst,
            send_sem=ssem.at[k],
            recv_sem=rsem.at[k],
            device_id=who,
            device_id_type=MESH,
        )
        copy.start()
        sent.append(copy)
        return copy

    total = jnp.zeros((1, width), F32)
    for c in range(6):
        x_copies[c].wait()
        total = total + jnp.sum(xv[c * chunk : (c + 1) * chunk, :], axis=0, keepdims=True)
    local = total * (1.0 / rows)
    mbuf[...] = jnp.zeros((8, B), F32)
    for i in range(nb):
        mbuf[i : i + 1, :] = local[:, i * B : (i + 1) * B]
    pl.semaphore_wait(barrier, len(everyone))

    slot = mx * 2 + mc
    near_copies = [send(mbuf, m_near.at[slot], who) for who in near]
    m_near[slot] = mbuf[...]

    for c in range(6):
        part = slice(c * chunk, (c + 1) * chunk)
        h, l = split(xv[part, :] - local)
        hi[part, :] = h
        lo[part, :] = l

    pairs = row_pairs(nb)
    own = (own0, own1, own2)
    core_in = (core0, core1, core2)
    a_in = (a_in0, a_in1, a_in2)
    part = [a.shape[2] for a in a_in]
    first = [sum(part[:k]) for k in range(len(part))]
    own_t = [o.reshape(2, 2, nx, n, B) for o, n in zip(own, part)]
    ta = sum(part)
    tb = b_in.shape[2]
    tz = z_in.shape[1]
    ax = [(x_peer, mx), (y_peer, my)]

    def near_mean():
        for copy in near_copies:
            copy.wait_recv()
        acc = m_near[0]
        for k in range(1, 2 * nx):
            acc = acc + m_near[k]
        return acc * (1.0 / (2 * nx))

    core_copies = []
    a_copies = []

    def scatter_a(k):
        core_copies[k].wait_recv()
        own_t[k][mc] = own_t[k][mc] + core_in[k][...]
        copies = [[], []]
        for d in range(1, nx):
            for q in range(2):
                peer, me = ax[q]
                to = lax.rem(me + d, nx)
                copies[q].append(send(own_t[k].at[mc, q, to], a_in[k].at[q, d - 1], peer(d)))
        a_copies.append(copies)

    for k, pair in enumerate(pairs):
        rs = slice(2 * B * k, 2 * B * (k + 1))
        rest = slice(2 * B * k, width)
        g = lax.dot_general(hi[:, rs], hi[:, rest], TT, preferred_element_type=F32)
        g += lax.dot_general(hi[:, rs], lo[:, rest], TT, preferred_element_type=F32)
        g += lax.dot_general(lo[:, rs], hi[:, rest], TT, preferred_element_type=F32)
        if k == 0:
            group = near_mean()
            m_far[mz, my] = group
            y_copies = [send(m_far.at[mz, my], m_far.at[mz, my], who) for who in y_peers]
            delta = mbuf[...] - group
            delta_t = delta.T * float(rows)
        for n, (i, j) in enumerate(pair):
            col = jnp.broadcast_to(delta_t[:, i : i + 1], (B, B))
            row = jnp.broadcast_to(delta[j : j + 1, :], (B, B))
            gi, gj = (i - 2 * k) * B, (j - 2 * k) * B
            own[k][n] = g[gi : gi + B, gj : gj + B] + col * row
        core_copies.append(send(own_t[k].at[1 - mc], core_in[k], core_peer))
        if k:
            scatter_a(k - 1)
    for copy in y_copies:
        copy.wait_recv()
    far_copies = [send(m_far.at[mz], m_far.at[mz], who) for who in z_peers]
    scatter_a(len(pairs) - 1)

    b_copies = [[], []]
    for q in range(2):
        me = ax[q][1]
        for k in range(len(pairs)):
            acc = own_t[k][mc, q, me]
            for d in range(1, nx):
                a_copies[k][q][d - 1].wait_recv()
                acc = acc + a_in[k][q, d - 1]
            b_own[q, first[k] : first[k] + part[k]] = acc
        b_own[q, ta:] = jnp.zeros((b_own.shape[1] - ta, B), F32)
        peer, me = ax[1 - q]
        for d in range(1, ny):
            k = lax.rem(me + d, ny)
            b_copies[q].append(
                send(
                    b_own.at[q, pl.ds(pl.multiple_of(k * tb, 8), tb)],
                    b_in.at[q, d - 1],
                    peer(d),
                )
            )
    for q in range(2):
        me = ax[1 - q][1]
        acc = b_own[q, pl.ds(pl.multiple_of(me * tb, 8), tb)]
        for d in range(1, ny):
            b_copies[q][d - 1].wait_recv()
            acc = acc + b_in[q, d - 1]
        z_own[q * tb : (q + 1) * tb] = acc
    z_own[2 * tb :] = jnp.zeros((z_own.shape[0] - 2 * tb, B), F32)
    z_copies = []
    for d in range(1, nz):
        k = lax.rem(mz + d, nz)
        z_copies.append(
            send(z_own.at[pl.ds(pl.multiple_of(k * tz, 8), tz)], z_in.at[d - 1], z_peer(d))
        )

    for copy in far_copies:
        copy.wait_recv()
    m_groups = m_far.reshape(nz * ny, 8, B)
    for i in range(nb):
        rows_i = m_groups[:, i, :]
        mean_i = jnp.sum(rows_i, axis=0, keepdims=True) * (1.0 / (nz * ny))
        mean_ref[:, i * B : (i + 1) * B] = mean_i
        dm[:, i * B : (i + 1) * B] = rows_i - mean_i

    acc = z_own[pl.ds(pl.multiple_of(mz * tz, 8), tz)]
    for d in range(1, nz):
        z_copies[d - 1].wait_recv()
        acc = acc + z_in[d - 1]
    mine = pl.ds(pl.multiple_of(mz * tz, 8), tz)
    z_all[mine] = acc
    z_copies = [send(z_all.at[mine], z_all.at[mine], who) for who in z_peers]

    for k, pair in enumerate(pairs):
        rs = slice(2 * B * k, 2 * B * (k + 1))
        rest = slice(2 * B * k, width)
        g = lax.dot_general(
            dm[:, rs], dm[:, rest], TT, precision=HI, preferred_element_type=F32
        ) * float(2 * nx * rows)
        for i, j in pair:
            gi, gj = (i - 2 * k) * B, (j - 2 * k) * B
            bmat[at[i, j]] = g[gi : gi + B, gj : gj + B]

    for c in z_copies:
        c.wait_recv()
    b_copies = [[], []]
    for q in range(2):
        peer, me = ax[1 - q]
        mine = pl.ds(pl.multiple_of(me * tb, 8), tb)
        src = z_all.at[q * tb : (q + 1) * tb]
        b_copies[q] = [send(src, b_all.at[q, mine], peer(d)) for d in range(1, ny)]
        b_all[q, mine] = z_all[q * tb : (q + 1) * tb]
    back = []
    gathers = []
    for dst, at_row, n in ((head, 0, part[0]), (tail, part[0], ta - part[0])):
        copies = [[], []]
        for q in range(2):
            if dst is head:
                for c in b_copies[q]:
                    c.wait_recv()
            peer, me = ax[q]
            src = b_all.at[q, at_row : at_row + n]
            copies[q] = [send(src, dst.at[mc, q, me], peer(d)) for d in range(1, nx)]
            back.append(send(src, dst.at[mc, q, me], core_peer))
            dst[mc, q, me] = b_all[q, at_row : at_row + n]
        gathers.append(copies)
    for dst, copies in zip((head, tail), gathers):
        for d in range(1, nx):
            for q in range(2):
                copies[q][d - 1].wait_recv()
                k = lax.rem(ax[q][1] + nx - d, nx)
                back.append(send(dst.at[mc, q, k], dst.at[mc, q, k], core_peer))
    for c in back:
        c.wait_recv()
    n_head = len(pairs[0])
    whole_head = head.reshape(n_head, B, B)
    for k in range(n_head):
        out_ref[k] = whole_head[k] + bmat[k]
    pieces = tail.reshape(4 * nx, ta - part[0], B)
    start = n_head
    for k in range(1, len(pairs)):
        for t in range(len(pairs[k]) * B // 8):
            piece, off = divmod(8 * t, part[k])
            off += first[k] - part[0]
            block, row = start + 8 * t // B, 8 * t % B
            out_ref[block, row : row + 8] = (
                pieces[piece, off : off + 8] + bmat[block, row : row + 8]
            )
        start += len(pairs[k])
    for c in sent:
        c.wait_send()


def summed_gram(dims, x):
    nx, ny, nz, width = dims
    rows = x.shape[0]
    nb = width // B
    n_blocks = nb * (nb + 1) // 2
    sizes = [len(pair) for pair in row_pairs(nb)]
    part = [n * B // (4 * nx) for n in sizes]
    ta = sum(part)
    tb = -(-ta // (8 * ny)) * 8
    tz = -(-2 * tb // (8 * nz)) * 8
    n_mean = 2 * nx - 1 + (ny - 1) + (nz - 1)
    n_copies = n_mean + 3 + 6 * (nx - 1) + 4 * (ny - 1) + 2 * (nz - 1) + 4 * (nx - 1) + 4 * nx
    vmem = pl.BlockSpec(memory_space=pltpu.VMEM)
    return pl.pallas_call(
        functools.partial(gram_kernel, dims),
        out_shape=(
            jax.ShapeDtypeStruct((n_blocks, B, B), F32),
            jax.ShapeDtypeStruct((1, width), F32),
        ),
        in_specs=[pl.BlockSpec(memory_space=pl.ANY)],
        out_specs=(vmem, vmem),
        scratch_shapes=[
            pltpu.VMEM((rows, width), F32),
            pltpu.VMEM((rows, width), BF16),
            pltpu.VMEM((rows, width), BF16),
            *[pltpu.VMEM((n, B, B), F32) for n in sizes],
            *[pltpu.VMEM((2, nx, n, B), F32) for n in part],
            *[pltpu.VMEM((2, nx - 1, n, B), F32) for n in part],
            pltpu.VMEM((2, 2, nx, part[0], B), F32),
            pltpu.VMEM((2, 2, nx, ta - part[0], B), F32),
            pltpu.VMEM((n_blocks, B, B), F32),
            pltpu.VMEM((2, tb * ny, B), F32),
            pltpu.VMEM((2, ny - 1, tb, B), F32),
            pltpu.VMEM((tz * nz, B), F32),
            pltpu.VMEM((nz - 1, tz, B), F32),
            pltpu.VMEM((tz * nz, B), F32),
            pltpu.VMEM((2, tb * ny, B), F32),
            pltpu.VMEM((8, B), F32),
            pltpu.VMEM((2 * nx, 8, B), F32),
            pltpu.VMEM((nz, ny, 8, B), F32),
            pltpu.VMEM((nz * ny, width), F32),
            pltpu.SemaphoreType.DMA((n_copies,)),
            pltpu.SemaphoreType.DMA((n_copies,)),
            pltpu.SemaphoreType.DMA((6,)),
        ],
        compiler_params=pltpu.CompilerParams(
            collective_id=0, has_side_effects=True, vmem_limit_bytes=56 << 20
        ),
        cost_estimate=pl.CostEstimate(
            flops=2 * rows * width * width, bytes_accessed=4 * rows * width, transcendentals=0
        ),
        name="summed_gram",
    )(x)


def rows_bcast(x, k):
    return jnp.broadcast_to(x[k : k + 1, :], (8, B))
def lane_bcast(x, c):
    return jnp.broadcast_to(x[:, c : c + 1], (8, B))


def factor_block(S, ones):
    lane = lax.broadcasted_iota(jnp.int32, (8, B), 1)
    sub = lax.broadcasted_iota(jnp.int32, (8, B), 0)
    S = list(S)
    out = []
    D = [lane_bcast(S[0], l) * ones for l in range(8)]
    for p in range(16):
        base = 8 * p
        inpanel = (lane >= base) & (lane < base + 8)
        C = D
        more = p < 15
        row_s = S[p]
        row_t = jnp.where(inpanel, jnp.where(lane == base + sub, 1.0, 0.0), S[p])
        if more:
            c = [lane_bcast(S[p + 1], base + j) * ones for j in range(8)]
            D = [lane_bcast(S[p + 1], base + 8 + l) * ones for l in range(8)]
            nxt = jnp.where(inpanel, 0.0, S[p + 1])
        pivot = rows_bcast(C[0], 0)
        diag = rdiag = None
        for j in range(8):
            r = 1.0 / pivot
            U = {l: rows_bcast(C[l], j) for l in range(j + 1, 8)}
            m = jnp.where(sub > j, C[j], 0.0) * r
            diag = pivot if j == 0 else jnp.where(sub == j, pivot, diag)
            rdiag = r if j == 0 else jnp.where(sub == j, r, rdiag)
            if j < 7:
                pivot = rows_bcast(C[j + 1], j + 1) - (U[j + 1] * U[j + 1]) * r
            for l in range(j + 1, 8):
                C[l] = C[l] - m * U[l]
            us = rows_bcast(row_s, j)
            ut = rows_bcast(row_t, j)
            row_s = row_s - m * us
            row_t = row_t - m * ut
            if more:
                e = c[j] * r
                for k in range(j + 1, 8):
                    c[k] = c[k] - e * U[k]
                for l in range(8):
                    D[l] = D[l] - e * rows_bcast(c[j], l)
                nxt = nxt - e * ut
        rs = lax.rsqrt(diag)
        out.append(jnp.where(lane > base + sub, row_s, row_t) * rs)
        if p < 14:
            Q = row_t * rdiag
            for l in range(7, 0, -1):
                Q = Q - (jnp.where(sub < l, C[l], 0.0) * rdiag) * rows_bcast(Q, l)
            q = [rows_bcast(Q, j) for j in range(8)]
            for i in range(p + 2, 16):
                acc = jnp.where(inpanel, 0.0, S[i])
                for j in range(8):
                    acc = acc - lane_bcast(S[i], base + j) * q[j]
                S[i] = acc
        if more:
            S[p + 1] = nxt
    return out

def factor_whiten_kernel(scale, g_ref, mean_ref, x_hbm, r_hbm, o_hbm, r_ref, w_ref, mh, ml, xv, hi, lo, o, xsem, osem, rsem, ones_ref):
    n = r_ref.shape[0]
    nb = n // B
    rows = xv.shape[0]
    CH = rows // 4
    xcopies = [pltpu.make_async_copy(x_hbm.at[c*CH:(c+1)*CH], xv.at[c*CH:(c+1)*CH], xsem.at[c]) for c in range(4)]
    for c in xcopies: c.start()
    for k, (i, j) in enumerate(tri_blocks(nb)):
        w_ref[i * B : (i + 1) * B, j * B : (j + 1) * B] = g_ref[k]
    li = lax.broadcasted_iota(jnp.int32, (B, B), 0)
    lj = lax.broadcasted_iota(jnp.int32, (B, B), 1)
    inv = 1.0 / scale

    def dot(a, b):
        return jnp.dot(a, b, precision=HI, preferred_element_type=F32)

    def dot_t(a, b):
        return lax.dot_general(a, b, TT, precision=HI, preferred_element_type=F32)

    def do_split(c):
        def f():
            if c % 4 == 0: xcopies[c // 4].wait()
            s = slice(c * CH // 4, (c + 1) * CH // 4)
            h, l = split(xv[s, :] - mean_ref[...])
            hi[s, :] = h
            lo[s, :] = l
        return f

    def do_whiten(pair, c):
        def f():
            s = slice(c * CH, (c + 1) * CH)
            top = 2 * B * (pair + 1)
            cs = slice(top - 2 * B, top)
            h = hi[s, :top]
            a = lax.dot_general(h, ml[cs, :top], NT, preferred_element_type=F32)
            a += lax.dot_general(lo[s, :top], mh[cs, :top], NT, preferred_element_type=F32)
            a += lax.dot_general(h, mh[cs, :top], NT, preferred_element_type=F32)
            o[s, cs] = a
            cp = pltpu.make_async_copy(o.at[s, cs], o_hbm.at[s, cs], osem.at[4 * pair + c])
            cp.start()
            ocopies.append(cp)

        return f

    ocopies = []
    ones_ref[...] = jnp.full((8, B), 1.0, F32)
    ones = ones_ref[...]
    work = [do_split(c) for c in range(16)]
    for b in range(nb):
        bs = slice(B * b, B * (b + 1))
        S = [w_ref[B * b + 8 * i : B * b + 8 * i + 8, bs] for i in range(16)]
        for i, t in enumerate(factor_block(S, ones)):
            w_ref[B * b + 8 * i : B * b + 8 * i + 8, bs] = t
        for f in work:
            f()
        F = w_ref[bs, bs]
        M = jnp.where(li >= lj, F, 0.0)
        before = slice(0, B * b)
        after = slice(B * (b + 1), n)
        nxt = slice(B * (b + 1), B * (b + 2))
        beyond = slice(B * (b + 2), n)
        if b < nb - 1:
            Rn = dot(M, w_ref[bs, nxt])
            w_ref[bs, nxt] = Rn
            w_ref[nxt, nxt] = w_ref[nxt, nxt] - dot_t(Rn, Rn)
        work = []

        def finish_row(b=b, bs=bs, before=before, beyond=beyond, after=after, M=M, F=F):
            if b > 0:
                w_ref[bs, before] = dot(M, w_ref[bs, before])
            if b < nb - 2:
                w_ref[bs, beyond] = dot(M, w_ref[bs, beyond])

        def outputs(b=b, bs=bs, nxt=nxt, before=before, after=after, M=M, F=F):
            R = jnp.where(li < lj, F, jnp.where(li == lj, 1.0 / F, 0.0))
            r_ref[bs, bs] = R * inv
            h, l = split(M * scale)
            mh[bs, bs] = h
            ml[bs, bs] = l
            if b > 0:
                r_ref[bs, before] = jnp.zeros((B, B * b), F32)
                h, l = split(w_ref[bs, before] * scale)
                mh[bs, before] = h
                ml[bs, before] = l
            if b < nb - 1:
                r_ref[bs, after] = w_ref[bs, after] * inv
            if b % 2 == 0:
                none = jnp.zeros((B, B), BF16)
                mh[bs, nxt] = none
                ml[bs, nxt] = none
            cp = pltpu.make_async_copy(r_ref.at[bs, :], r_hbm.at[bs, :], rsem.at[b])
            cp.start()
            ocopies.append(cp)

        def update_next(b=b, bs=bs, nxt=nxt, before=before, beyond=beyond, M=M):
            Rn = w_ref[bs, nxt]
            if b < nb - 2:
                w_ref[nxt, beyond] = w_ref[nxt, beyond] - dot_t(Rn, w_ref[bs, beyond])
            if b > 0:
                w_ref[nxt, before] = w_ref[nxt, before] - dot_t(Rn, w_ref[bs, before])
            w_ref[nxt, bs] = -dot_t(Rn, M)

        def update_beyond(b=b, bs=bs, before=before, beyond=beyond, M=M):
            Ra = w_ref[bs, beyond]
            w_ref[beyond, beyond] = w_ref[beyond, beyond] - dot_t(Ra, Ra)
            if b > 0:
                w_ref[beyond, before] = w_ref[beyond, before] - dot_t(Ra, w_ref[bs, before])
            w_ref[beyond, bs] = -dot_t(Ra, M)

        work.append(finish_row)
        work.append(outputs)
        if b < nb - 1:
            work.append(update_next)
        if b < nb - 2:
            work.append(update_beyond)
        if b % 2:
            work += [do_whiten(b // 2, c) for c in range(4)]
    for f in work:
        f()
    for c in ocopies:
        c.wait()

def factor_whiten(gram, mean, x, scale):
    rows, width = x.shape
    vmem = pl.BlockSpec(memory_space=pltpu.VMEM)
    hbm = pl.BlockSpec(memory_space=pl.ANY)
    return pl.pallas_call(
        functools.partial(factor_whiten_kernel, scale),
        out_shape=(
            jax.ShapeDtypeStruct((width, width), F32),
            jax.ShapeDtypeStruct((rows, width), F32),
        ),
        in_specs=[vmem, vmem, hbm],
        out_specs=(hbm, hbm),
        scratch_shapes=[pltpu.VMEM((width, width), F32), pltpu.VMEM((width, width), F32), pltpu.VMEM((width, width), BF16), pltpu.VMEM((width, width), BF16),
            pltpu.VMEM((rows, width), F32), pltpu.VMEM((rows, width), BF16), pltpu.VMEM((rows, width), BF16), pltpu.VMEM((rows, width), F32),
            pltpu.SemaphoreType.DMA((4,)), pltpu.SemaphoreType.DMA((2 * width // B,)), pltpu.SemaphoreType.DMA((width // B,)), pltpu.VMEM((8, B), F32)],
        compiler_params=pltpu.CompilerParams(vmem_limit_bytes=56 << 20),
        name="factor_whiten",
    )(gram, mean, x)


def shards(dims, row_count, embeddings):
    gram, mean = summed_gram(dims, embeddings)
    r, whitened = factor_whiten(gram, mean, embeddings, math.sqrt(row_count))
    return whitened, r


def solution(mesh):
    nx = mesh.shape["grp"]
    ny = 4
    nz = mesh.shape["wide"] // (2 * ny)

    def whole(embeddings):
        rows, width = embeddings.shape
        return jax.shard_map(
            functools.partial(shards, (nx, ny, nz, width), rows),
            mesh=mesh,
            in_specs=(P(("grp", "wide"), None),),
            out_specs=(P(("grp", "wide"), None), P()),
            check_vma=False,
        )(embeddings)

    return whole
```
